32 devices in a mesh: nodes: 8 (over y, x, core), cols: 4 (over z).
Axes of the slice: x: 2, y: 2, z: 4, core: 2. Of those that a mesh axis runs over, the one named last changes fastest.
Arguments:
- prior: float32 [65536, 128], P(('nodes', 'cols')), may hold values from -18 to 18
- queries: int32 [128], replicated, may hold values from 0 to 65535
- tile_rows: int32 [2048], P(('nodes', 'cols')), may hold values from -1 to 511, as said below
- tile_cols: int32 [2048], P(('nodes', 'cols')), may hold values from -1 to 511
- tile_ids: int32 [2048, 8, 128], P(('nodes', 'cols')), may hold values from 0 to 127
- tile_weights: float32 [2048, 8, 128], P(('nodes', 'cols')), may hold values from 0.1 to 1
Outputs:
- solution: float32 [65536, 128], P(('nodes', 'cols'))
- residual: float32 [65536, 128], P(('nodes', 'cols'))
The draws below stay inside these ranges and needn't reach their ends.
Inputs may be any that keep to these rules, and one draw needn't show every extreme that they name: Tiles come in 8 node groups of 64 consecutive row blocks; the slots of the devices of group g hold only tiles with row blocks in group g. A live tile's column block is at most 4 blocks from its row block; every block's diagonal tile is present; no block pair appears twice. An empty slot has -1 in both tile_rows and tile_cols.
All inputs are finite; a program needn't handle non-finite values.
Results may differ from the reference program's by a relative error of at most 0.0017.
Values sent between devices are 32-bit elements; how exact they have to be, the bound alone decides.
A program may use at most 128 MiB of HBM per device.

```python
import math
import jax
import jax.numpy as jnp
from jax import lax

TB = 128
Q = 128
KT = 8
BAND = 4
ITERS = 3
BLOCKS = 64
TILE_DEV = 64
NBLK = 512
NODES = 65536
TILES = 2048
N_NODES = 8
N_COLS = 4


def tile_layout(key):
    band_width = 2 * BAND + 1
    pairs = BLOCKS * band_width
    per_group = TILE_DEV * N_COLS

    def one_group(group_id):
        order_rank = jax.random.permutation(jax.random.fold_in(key, group_id), pairs).astype(jnp.int32)
        pair_index = jnp.arange(pairs, dtype=jnp.int32)
        offset = pair_index % band_width - BAND
        scores = order_rank - pairs * (offset == 0).astype(jnp.int32)
        chosen = jnp.argsort(scores, stable=True)[:per_group].astype(jnp.int32)
        row_block = chosen // band_width
        col_block = row_block + chosen % band_width - BAND
        glob_row = group_id * BLOCKS + row_block
        glob_col = group_id * BLOCKS + col_block
        inside = (glob_col >= 0) & (glob_col < NBLK)
        return (jnp.where(inside, glob_row, -1), jnp.where(inside, glob_col, -1))
    row_all, col_all = jax.vmap(one_group)(jnp.arange(N_NODES, dtype=jnp.int32))
    row_all = row_all.reshape(N_NODES, TILE_DEV, N_COLS).transpose(0, 2, 1).reshape(-1)
    col_all = col_all.reshape(N_NODES, TILE_DEV, N_COLS).transpose(0, 2, 1).reshape(-1)
    return (row_all.astype(jnp.int32), col_all.astype(jnp.int32))


def draw_tile_rows(key, part):
    return tile_layout(jax.random.fold_in(key, 11))[0]


def draw_tile_cols(key, part):
    return tile_layout(jax.random.fold_in(key, 11))[1]


def draw_prior(key, part):
    position = jnp.arange(NODES, dtype=jnp.float32)[:, None] / NODES
    rise_row = 1.0 + 2.0 * position
    base_draw = jax.random.normal(jax.random.fold_in(key, 1), (NODES, Q), jnp.float32)
    return jnp.clip(base_draw, -4.0, 4.0) * rise_row


def with_ends(array, own_key, low, largest):
    shape = array.shape
    spot = [jax.random.randint(jax.random.fold_in(own_key, axis), (), 0, shape[axis]) for axis in range(len(shape))]
    array = array.at[tuple(spot)].set(low)
    longest = shape.index(max(shape))
    spot[longest] = (spot[longest] + 1) % shape[longest]
    return array.at[tuple(spot)].set(largest)


def level_of(own_key, extent, split, smallest, largest):
    loudness = 1.0
    for dim, blocks in split:
        steps = jax.random.uniform(jax.random.fold_in(jax.random.fold_in(own_key, 6), dim), (blocks,), jnp.float32, smallest / len(split), largest / len(split))
        loudness = loudness * jnp.repeat(jnp.exp(steps), extent[dim] // blocks).reshape((-1,) + (1,) * (len(extent) - 1 - dim))
    return loudness


def setup_inputs(seed: int = 0) -> dict:
    key_list = jax.random.split(jax.random.key(seed), 7)
    prior = draw_prior(jax.random.fold_in(key_list[6], 71), 0)
    queries = with_ends(jax.random.randint(key_list[1], (Q,), 0, NODES), jax.random.fold_in(key_list[1], 1), 0, NODES - 1).astype(jnp.int32)
    tile_rows = draw_tile_rows(jax.random.fold_in(key_list[6], 71), 0)
    tile_cols = draw_tile_cols(jax.random.fold_in(key_list[6], 71), 0)
    tile_ids = with_ends(jax.random.randint(key_list[4], (TILES, KT, TB), 0, TB), jax.random.fold_in(key_list[4], 1), 0, TB - 1).astype(jnp.int32)
    tile_weights = jnp.clip(jnp.exp(math.log(1.0) - 2.3025851 * jax.random.uniform(key_list[5], (TILES, KT, TB), jnp.float32) ** level_of(key_list[5], (TILES, KT, TB), ((0, 32),), -0.2, 0.2)), 0.1, 1.0)
    return {"prior": prior, "queries": queries, "tile_rows": tile_rows, "tile_cols": tile_cols, "tile_ids": tile_ids, "tile_weights": tile_weights}


HIGH = lax.Precision.HIGHEST
ALPHA = 0.9
BOOST = 4.0

def dense_tiles(tile_ids, tile_weights):
    columns = jnp.arange(TB, dtype=jnp.int32)
    total_sum = jnp.zeros((tile_ids.shape[0], TB, TB), jnp.float32)
    for slot_index in range(KT):
        matched = (tile_ids[:, slot_index, :, None] == columns[None, None, :]).astype(jnp.float32)
        total_sum = total_sum + tile_weights[:, slot_index, :, None] * matched
    return total_sum

def tile_items(tile_rows, tile_cols, tile_ids, tile_weights):
    return (tile_rows.reshape(-1, TILE_DEV), tile_cols.reshape(-1, TILE_DEV), tile_ids.reshape(-1, TILE_DEV, KT, TB), tile_weights.reshape(-1, TILE_DEV, KT, TB))

def unpack(item_set):
    row_block, col_block, ids_part, weights = item_set
    live_slot = row_block >= 0
    dense_tile = dense_tiles(ids_part, weights) * live_slot.astype(jnp.float32)[:, None, None]
    row_safe = jnp.where(live_slot, row_block, 0).astype(jnp.int32)
    col_safe = jnp.where(live_slot, col_block, 0).astype(jnp.int32)
    return (dense_tile, row_safe, col_safe)

def graph_degree(tile_rows, tile_cols, tile_ids, tile_weights):

    def tile_step(accumulated, item_set):
        dense_tile, row_safe, col_safe = unpack(item_set)
        accumulated = accumulated.at[row_safe].add(lax.optimization_barrier(jnp.sum(dense_tile, axis=2)))
        accumulated = accumulated.at[col_safe].add(lax.optimization_barrier(jnp.sum(dense_tile, axis=1)))
        return (accumulated, None)
    result, _ = lax.scan(tile_step, jnp.zeros((NBLK, TB), jnp.float32), tile_items(tile_rows, tile_cols, tile_ids, tile_weights))
    return result.reshape(NODES)

def graph_pass(vectors, tile_rows, tile_cols, tile_ids, tile_weights):
    query_width = vectors.shape[1]
    pieces = vectors.reshape(NBLK, TB, query_width)

    def tile_step(accumulated, item_set):
        dense_tile, row_safe, col_safe = unpack(item_set)
        forward = jnp.einsum('trj,tjq->trq', dense_tile, pieces[col_safe], precision=HIGH)
        backward = jnp.einsum('tjr,tjq->trq', dense_tile, pieces[row_safe], precision=HIGH)
        return (accumulated.at[row_safe].add(forward).at[col_safe].add(backward), None)
    result, _ = lax.scan(tile_step, jnp.zeros_like(pieces), tile_items(tile_rows, tile_cols, tile_ids, tile_weights))
    return result.reshape(NODES, query_width)

def inner_gram(left_vec, right_vec):
    return jnp.einsum('nq,np->qp', left_vec, right_vec, precision=HIGH)

def solve_gram(matrix, right_side):
    return jax.scipy.linalg.cho_solve((jnp.linalg.cholesky(matrix), True), right_side)

def reference(prior, queries, tile_rows, tile_cols, tile_ids, tile_weights):
    degree = graph_degree(tile_rows, tile_cols, tile_ids, tile_weights)
    inv_root = lax.rsqrt(degree)[:, None]
    node_ids = jnp.arange(NODES, dtype=jnp.int32)
    target = prior + BOOST * (node_ids[:, None] == queries[None, :]).astype(jnp.float32)
    solution = jnp.zeros_like(target)
    residual = target
    direction = target
    gram = inner_gram(residual, residual)
    for _ in range(ITERS):
        image_vec = direction - ALPHA * inv_root * graph_pass(inv_root * direction, tile_rows, tile_cols, tile_ids, tile_weights)
        curvature = inner_gram(direction, image_vec)
        step_mat = solve_gram(curvature, gram)
        solution = solution + jnp.dot(direction, step_mat, precision=HIGH)
        residual = residual - jnp.dot(image_vec, step_mat, precision=HIGH)
        gram_new = inner_gram(residual, residual)
        ratio_mat = solve_gram(gram, gram_new)
        direction = residual + jnp.dot(direction, ratio_mat, precision=HIGH)
        gram = gram_new
    return (solution, residual)
```

```python
import functools

import jax
import jax.numpy as jnp
from jax import lax
from jax.experimental import pallas as pl
from jax.experimental.pallas import tpu as pltpu
from jax.sharding import PartitionSpec as P

TB = 128
KT = 8
BAND = 4
ITERS = 3
SPAN = 2 * BAND + 1
HALO = BAND * TB
EDGE = BAND * (BAND + 1) // 2

HIGH = lax.Precision.HIGHEST
ALPHA = 0.9
BOOST = 4.0
MESH = pl.DeviceIdType.MESH


def mm(left, right):
    return jnp.dot(left, right, precision=HIGH, preferred_element_type=jnp.float32)


def mm_t(left, right):
    return lax.dot_general(
        left, right, (((0,), (0,)), ((), ())), precision=HIGH, preferred_element_type=jnp.float32
    )


def band_kernel(offsets, tiles_ref, band_ref, inv_ref):
    row = pl.program_id(0)
    places = lax.broadcasted_iota(jnp.int32, (TB, TB), 0).astype(jnp.float32)

    def transposed_tile(offset):
        at = pl.multiple_of(offset, 8)
        ids = tiles_ref[pl.ds(at, KT), :]
        weights = tiles_ref[pl.ds(at + KT, KT), :]
        total = jnp.zeros((TB, TB), jnp.float32)
        for k in range(KT):
            total = total + jnp.where(ids[k : k + 1, :] == places, weights[k : k + 1, :], 0.0)
        return total

    for o in range(SPAN):
        forward = offsets[0, row * SPAN + o]
        backward = offsets[1, row * SPAN + o]
        lanes = slice(o * TB, (o + 1) * TB)

        @pl.when(forward >= 0)
        def _():
            band_ref[:, lanes] = transposed_tile(forward).T

        @pl.when(forward < 0)
        def _():
            band_ref[:, lanes] = jnp.zeros((TB, TB), jnp.float32)

        @pl.when(backward >= 0)
        def _():
            band_ref[:, lanes] += transposed_tile(backward)

    folded = band_ref[:, 0:TB]
    for o in range(1, SPAN):
        folded = folded + band_ref[:, o * TB : (o + 1) * TB]
    degree = jnp.broadcast_to(jnp.sum(folded, axis=1, keepdims=True), (TB, TB))
    root = lax.rsqrt(degree)
    inv_ref[...] = root * (1.5 - 0.5 * degree * root * root)


def build_band(offsets, tiles, row_blocks):
    return pl.pallas_call(
        band_kernel,
        grid_spec=pltpu.PrefetchScalarGridSpec(
            num_scalar_prefetch=1,
            grid=(row_blocks,),
            in_specs=[pl.BlockSpec(tiles.shape, lambda i, _: (0, 0))],
            out_specs=[
                pl.BlockSpec((TB, SPAN * TB), lambda i, _: (i, 0)),
                pl.BlockSpec((TB, TB), lambda i, _: (i, 0)),
            ],
        ),
        out_shape=[
            jax.ShapeDtypeStruct((row_blocks * TB, SPAN * TB), jnp.float32),
            jax.ShapeDtypeStruct((row_blocks * TB, TB), jnp.float32),
        ],
        compiler_params=pltpu.CompilerParams(vmem_limit_bytes=32 * 1024 * 1024),
    )(offsets, tiles)


def flipped(index, bit):
    return index + bit - 2 * bit * ((index // bit) % 2)


def cg_kernel(
    nodes, cols, prior_ref, queries_ref, band_ref, inv_ref, x_ref, r_ref,
    vext, direc, image, wbuf, acc, slots, pair, curv_old, ratio_ref, step_ref,
    halo_send, halo_recv, sum_send, sum_recv,
):
    rows = prior_ref.shape[0]
    blocks = rows // TB
    node = lax.axis_index("nodes")
    col = lax.axis_index("cols")
    right = ((node + (col + 1) // cols) % nodes, (col + 1) % cols)
    left = ((node + nodes - 1 + (col + cols - 1) // cols) % nodes, (col + cols - 1) % cols)
    partners = []
    bit = 1
    while bit < nodes:
        partners.append((flipped(node, bit), col))
        bit *= 2
    bit = 1
    while bit < cols:
        partners.append((node, flipped(col, bit)))
        bit *= 2
    stages = len(partners)

    barrier = pltpu.get_barrier_semaphore()
    for other in [left, right] + partners:
        pl.semaphore_signal(barrier, inc=1, device_id=other, device_id_type=MESH)

    base = (node * cols + col) * rows
    chunk = 2 * TB

    def start_rows(c, carry):
        at = pl.ds(pl.multiple_of(c * chunk, chunk), chunk)
        where_at = base + c * chunk + lax.broadcasted_iota(jnp.int32, (chunk, TB), 0)
        r_ref[at, :] = prior_ref[at, :] + jnp.where(where_at == queries_ref[...], BOOST, 0.0)
        x_ref[at, :] = jnp.zeros((chunk, TB), jnp.float32)
        direc[at, :] = jnp.zeros((chunk, TB), jnp.float32)
        image[at, :] = jnp.zeros((chunk, TB), jnp.float32)
        return carry

    lax.fori_loop(0, rows // chunk, start_rows, 0)
    pair[...] = jnp.zeros_like(pair)
    curv_old[...] = jnp.zeros_like(curv_old)
    lane = lax.broadcasted_iota(jnp.int32, (TB, TB), 1)
    lane_row = lax.broadcasted_iota(jnp.int32, (1, TB), 1)
    pl.semaphore_wait(barrier, stages + 2)

    def iteration(it, carry):
        def scale_rows(c, inner):
            at = pl.multiple_of(c * chunk, chunk)
            vext[it, pl.ds(HALO + at, chunk), :] = inv_ref[pl.ds(at, chunk), :] * r_ref[pl.ds(at, chunk), :]
            return inner

        lax.fori_loop(0, rows // chunk, scale_rows, 0)
        to_right = pltpu.make_async_remote_copy(
            src_ref=vext.at[it, pl.ds(rows, HALO), :],
            dst_ref=vext.at[it, pl.ds(0, HALO), :],
            send_sem=halo_send.at[2 * it], recv_sem=halo_recv.at[2 * it],
            device_id=right, device_id_type=MESH,
        )
        to_left = pltpu.make_async_remote_copy(
            src_ref=vext.at[it, pl.ds(HALO, HALO), :],
            dst_ref=vext.at[it, pl.ds(HALO + rows, HALO), :],
            send_sem=halo_send.at[2 * it + 1], recv_sem=halo_recv.at[2 * it + 1],
            device_id=left, device_id_type=MESH,
        )
        to_right.start()
        to_left.start()

        def apply_block(b, inner):
            at = pl.multiple_of(b * TB, TB)
            product = mm(band_ref[pl.ds(at, TB), :], vext[it, pl.ds(at, SPAN * TB), :])
            mine = pl.ds(at, TB)
            wbuf[mine, :] = r_ref[mine, :] - ALPHA * inv_ref[mine, :] * product
            return inner

        lax.fori_loop(BAND, blocks - BAND, apply_block, 0)
        to_right.wait()
        to_left.wait()
        lax.fori_loop(0, BAND, apply_block, 0)
        lax.fori_loop(blocks - BAND, blocks, apply_block, 0)

        acc[...] = jnp.zeros_like(acc)

        def add_gram(c, inner):
            at = pl.ds(pl.multiple_of(c * chunk, chunk), chunk)
            part = r_ref[at, :]
            acc[...] += mm_t(part, jnp.concatenate([part, wbuf[at, :]], axis=1))
            return inner

        lax.fori_loop(0, rows // chunk, add_gram, 0)
        for stage, other in enumerate(partners):
            spot = it * stages + stage
            copy = pltpu.make_async_remote_copy(
                src_ref=acc, dst_ref=slots.at[spot],
                send_sem=sum_send.at[spot], recv_sem=sum_recv.at[spot],
                device_id=other, device_id_type=MESH,
            )
            copy.start()
            copy.wait()
            acc[...] += slots[spot]

        gram = acc[:, 0:TB]
        ratio = mm(pair[0], gram)
        ratio_ref[...] = ratio
        curvature = acc[:, TB : 2 * TB] - mm_t(ratio, mm(curv_old[...], ratio))
        curv_old[...] = curvature
        pair[0] = gram
        pair[1] = curvature

        def pivot(k, inner):
            for j in range(2):
                whole = pair[j]
                line = pair[j, pl.ds(k, 1), :]
                hit = lane == k
                hit_row = lane_row == k
                column = jnp.sum(jnp.where(hit, whole, 0.0), axis=1, keepdims=True)
                corner = jnp.sum(jnp.where(hit_row, line, 0.0), axis=1, keepdims=True)
                scaled = jnp.where(hit_row, 1.0, line) / corner
                pair[j] = jnp.where(hit, 0.0, whole) - column * scaled
                pair[j, pl.ds(k, 1), :] = scaled
            return inner

        lax.fori_loop(0, TB, pivot, 0)
        step_ref[...] = mm(pair[1], acc[:, 0:TB])

        def update_rows(c, inner):
            at = pl.ds(pl.multiple_of(c * chunk, chunk), chunk)
            fresh = r_ref[at, :] + mm(direc[at, :], ratio_ref[...])
            direc[at, :] = fresh
            x_ref[at, :] += mm(fresh, step_ref[...])
            turned = wbuf[at, :] + mm(image[at, :], ratio_ref[...])
            image[at, :] = turned
            r_ref[at, :] -= mm(turned, step_ref[...])
            return inner

        lax.fori_loop(0, rows // chunk, update_rows, 0)
        return carry

    lax.fori_loop(0, ITERS, iteration, 0)


def run_cg(nodes, cols, prior, queries, band, inv):
    rows = prior.shape[0]
    stages = (nodes.bit_length() - 1) + (cols.bit_length() - 1)
    full = pl.BlockSpec(memory_space=pltpu.VMEM)
    shape = jax.ShapeDtypeStruct((rows, TB), jnp.float32)
    big = pltpu.VMEM((rows, TB), jnp.float32)
    small = pltpu.VMEM((TB, TB), jnp.float32)
    return pl.pallas_call(
        functools.partial(cg_kernel, nodes, cols),
        in_specs=[full] * 4,
        out_specs=[full] * 2,
        out_shape=[shape, shape],
        scratch_shapes=[
            pltpu.VMEM((ITERS, rows + 2 * HALO, TB), jnp.float32),
            big, big, big,
            pltpu.VMEM((TB, 2 * TB), jnp.float32),
            pltpu.VMEM((ITERS * stages, TB, 2 * TB), jnp.float32),
            pltpu.VMEM((2, TB, TB), jnp.float32),
            small, small, small,
            pltpu.SemaphoreType.DMA((2 * ITERS,)),
            pltpu.SemaphoreType.DMA((2 * ITERS,)),
            pltpu.SemaphoreType.DMA((ITERS * stages,)),
            pltpu.SemaphoreType.DMA((ITERS * stages,)),
        ],
        compiler_params=pltpu.CompilerParams(
            collective_id=0, has_side_effects=True, vmem_limit_bytes=56 * 1024 * 1024
        ),
    )(prior, queries, band, inv)


def body(prior, queries, tile_rows, tile_cols, tile_ids, tile_weights):
    rows_dev = prior.shape[0]
    nodes = lax.axis_size("nodes")
    cols = lax.axis_size("cols")
    node = lax.axis_index("nodes")
    member = lax.axis_index("cols")
    per_dev = tile_rows.shape[0]
    row_blocks = rows_dev // TB
    blocks = row_blocks * cols
    first = node * blocks

    keys = jnp.where(
        tile_rows >= 0, (tile_rows - first) * SPAN + (tile_cols - tile_rows + BAND), -1
    ).astype(jnp.float32)
    packed = jnp.concatenate([tile_ids.astype(jnp.float32), tile_weights], axis=1)
    meta_rows = 8 * (-(-per_dev // (8 * TB)))
    meta = jnp.full((meta_rows * TB,), -1.0, jnp.float32).at[:per_dev].set(keys)
    flat = jnp.concatenate([packed.reshape(per_dev * 2 * KT, TB), meta.reshape(meta_rows, TB)])
    gathered = lax.all_gather(flat, "cols", axis=0, tiled=False)
    stride = flat.shape[0]
    slot_keys = gathered[:, per_dev * 2 * KT :, :].reshape(cols, -1)[:, :per_dev].reshape(-1).astype(jnp.int32)
    slot = jnp.arange(cols * per_dev, dtype=jnp.int32)
    slot_at = (slot // per_dev) * stride + (slot % per_dev) * 2 * KT

    def find(wanted):
        return jnp.max(
            jnp.where(wanted[:, None] == slot_keys[None, :], slot_at[None, :], -1), axis=1
        )

    far = [a for a in range(BAND) for _ in range(a + 1)]
    near = [c for a in range(BAND) for c in range(a + 1)]
    far = jnp.array(far, jnp.int32)
    near = jnp.array(near, jnp.int32)
    up_keys = (blocks - BAND + far) * SPAN + (2 * BAND + near - far)
    down_keys = near * SPAN + (far - near)
    group_tiles = gathered.reshape(cols * stride, TB)

    def pick(wanted):
        at = find(wanted)
        found = jnp.maximum(at, 0)[:, None] + jnp.arange(2 * KT, dtype=jnp.int32)[None, :]
        chosen = group_tiles[found]
        return jnp.where((at >= 0)[:, None, None], chosen, 0.0).reshape(EDGE * 2 * KT, TB)

    from_prev = lax.ppermute(pick(up_keys), "nodes", [(i, i + 1) for i in range(nodes - 1)])
    from_next = lax.ppermute(pick(down_keys), "nodes", [(i + 1, i) for i in range(nodes - 1)])
    tiles = jnp.concatenate([group_tiles, from_prev, from_next])

    place = jnp.arange(row_blocks * SPAN, dtype=jnp.int32)
    i_at = member * row_blocks + place // SPAN
    o_at = place % SPAN
    forward = find(i_at * SPAN + o_at)
    back_row = i_at + o_at - BAND
    inside = find(back_row * SPAN + 2 * BAND - o_at)
    edge_at = cols * stride
    a_prev = back_row + BAND
    prev_at = edge_at + (a_prev * (a_prev + 1) // 2 + i_at) * 2 * KT
    c_next = i_at - (blocks - BAND)
    next_at = edge_at + (EDGE + c_next * (c_next + 1) // 2 + back_row - blocks) * 2 * KT
    backward = jnp.where(back_row < 0, prev_at, jnp.where(back_row >= blocks, next_at, inside))
    band, inv = build_band(jnp.stack([forward, backward]), tiles, row_blocks)
    return tuple(run_cg(nodes, cols, prior, queries[None, :], band, inv))


def solution(mesh):
    in_specs = (
        P(("nodes", "cols"), None),
        P(),
        P(("nodes", "cols")),
        P(("nodes", "cols")),
        P(("nodes", "cols"), None, None),
        P(("nodes", "cols"), None, None),
    )
    out_specs = (P(("nodes", "cols"), None), P(("nodes", "cols"), None))
    return jax.shard_map(body, mesh=mesh, in_specs=in_specs, out_specs=out_specs, check_vma=False)
```

```python
import functools

import jax
import jax.numpy as jnp
from jax import lax
from jax.experimental import pallas as pl
from jax.experimental.pallas import tpu as pltpu
from jax.sharding import PartitionSpec as P

TB = 128
KT = 8
BAND = 4
ITERS = 3
SPAN = 2 * BAND + 1
HALO = BAND * TB
EDGE = BAND * (BAND + 1) // 2

HIGH = lax.Precision.HIGHEST
ALPHA = 0.9
BOOST = 4.0
MESH = pl.DeviceIdType.MESH


def mm(left, right):
    return jnp.dot(left, right, precision=HIGH, preferred_element_type=jnp.float32)


def mm_t(left, right):
    return lax.dot_general(
        left, right, (((0,), (0,)), ((), ())), precision=HIGH, preferred_element_type=jnp.float32
    )


def band_kernel(offsets, tiles_ref, band_ref, inv_ref):
    row = pl.program_id(0)
    places = lax.broadcasted_iota(jnp.int32, (TB, TB), 0).astype(jnp.float32)

    def transposed_tile(offset):
        at = pl.multiple_of(offset, 8)
        ids = tiles_ref[pl.ds(at, KT), :]
        weights = tiles_ref[pl.ds(at + KT, KT), :]
        total = jnp.zeros((TB, TB), jnp.float32)
        for k in range(KT):
            total = total + jnp.where(ids[k : k + 1, :] == places, weights[k : k + 1, :], 0.0)
        return total

    for o in range(SPAN):
        forward = offsets[0, row * SPAN + o]
        backward = offsets[1, row * SPAN + o]
        lanes = slice(o * TB, (o + 1) * TB)

        @pl.when(forward >= 0)
        def _():
            band_ref[:, lanes] = transposed_tile(forward).T

        @pl.when(forward < 0)
        def _():
            band_ref[:, lanes] = jnp.zeros((TB, TB), jnp.float32)

        @pl.when(backward >= 0)
        def _():
            band_ref[:, lanes] += transposed_tile(backward)

    folded = band_ref[:, 0:TB]
    for o in range(1, SPAN):
        folded = folded + band_ref[:, o * TB : (o + 1) * TB]
    degree = jnp.broadcast_to(jnp.sum(folded, axis=1, keepdims=True), (TB, TB))
    root = lax.rsqrt(degree)
    inv_ref[...] = root * (1.5 - 0.5 * degree * root * root)


def build_band(offsets, tiles, row_blocks):
    return pl.pallas_call(
        band_kernel,
        grid_spec=pltpu.PrefetchScalarGridSpec(
            num_scalar_prefetch=1,
            grid=(row_blocks,),
            in_specs=[pl.BlockSpec(tiles.shape, lambda i, _: (0, 0))],
            out_specs=[
                pl.BlockSpec((TB, SPAN * TB), lambda i, _: (i, 0)),
                pl.BlockSpec((TB, TB), lambda i, _: (i, 0)),
            ],
        ),
        out_shape=[
            jax.ShapeDtypeStruct((row_blocks * TB, SPAN * TB), jnp.float32),
            jax.ShapeDtypeStruct((row_blocks * TB, TB), jnp.float32),
        ],
        compiler_params=pltpu.CompilerParams(vmem_limit_bytes=32 * 1024 * 1024),
    )(offsets, tiles)


def invert_in_place(matrix):
    lane = lax.broadcasted_iota(jnp.int32, (TB, TB), 1)
    lane_row = lax.broadcasted_iota(jnp.int32, (1, TB), 1)

    def entry(line, k):
        return jnp.sum(jnp.where(lane_row == k, line, 0.0), axis=1, keepdims=True)

    def pivot(m, carry):
        k = 2 * m
        whole = matrix[...]
        first = matrix[pl.ds(k, 1), :]
        second = matrix[pl.ds(k + 1, 1), :]
        hit0 = lane == k
        hit1 = lane == k + 1
        column0 = jnp.sum(jnp.where(hit0, whole, 0.0), axis=1, keepdims=True)
        column1 = jnp.sum(jnp.where(hit1, whole, 0.0), axis=1, keepdims=True)
        rest = jnp.where(hit0 | hit1, 0.0, whole)
        a = entry(first, k)
        b = entry(first, k + 1)
        c = entry(second, k)
        d = entry(second, k + 1)
        inv_a = 1.0 / a
        lower = c * inv_a
        upper = b * inv_a
        inv_s = 1.0 / (d - c * upper)
        row0 = jnp.where(lane_row == k, 1.0, jnp.where(lane_row == k + 1, 0.0, first))
        row1 = jnp.where(lane_row == k, 0.0, jnp.where(lane_row == k + 1, 1.0, second))
        new1 = (row1 - lower * row0) * inv_s
        new0 = row0 * inv_a - upper * new1
        matrix[...] = rest - column0 * new0 - column1 * new1
        matrix[pl.ds(k, 1), :] = new0
        matrix[pl.ds(k + 1, 1), :] = new1
        return carry

    lax.fori_loop(0, TB // 2, pivot, 0)


def cg_kernel(
    nodes, cols, prior_ref, queries_ref, band_ref, inv_ref, x_ref, r_ref,
    vext, direc, image, wbuf, acc, spread, column_sums, total, gram_inv, curv_inv, curv_old,
    ratio_ref, step_ref, halo_send, halo_recv, spread_send, spread_recv, col_send, col_recv,
    back_send, back_recv,
):
    rows = prior_ref.shape[0]
    blocks = rows // TB
    node = lax.axis_index("nodes")
    col = lax.axis_index("cols")
    right = ((node + (col + 1) // cols) % nodes, (col + 1) % cols)
    left = ((node + nodes - 1 + (col + cols - 1) // cols) % nodes, (col + cols - 1) % cols)
    share = 2 * TB // nodes

    def node_at(k):
        return (node + k) % nodes

    def col_at(k):
        return (col + k) % cols

    barrier = pltpu.get_barrier_semaphore()
    others = [left, right]
    others += [(node_at(k), col) for k in range(1, nodes)]
    others += [(node, col_at(k)) for k in range(1, cols)]
    for other in others:
        pl.semaphore_signal(barrier, inc=1, device_id=other, device_id_type=MESH)

    base = (node * cols + col) * rows
    chunk = 2 * TB

    def start_rows(c, carry):
        start = pl.multiple_of(c * chunk, chunk)
        at = pl.ds(start, chunk)
        where_at = base + c * chunk + lax.broadcasted_iota(jnp.int32, (chunk, TB), 0)
        target = prior_ref[at, :] + jnp.where(where_at == queries_ref[...], BOOST, 0.0)
        r_ref[at, :] = target
        vext[0, pl.ds(HALO + start, chunk), :] = inv_ref[at, :] * target
        x_ref[at, :] = jnp.zeros((chunk, TB), jnp.float32)
        direc[at, :] = jnp.zeros((chunk, TB), jnp.float32)
        image[at, :] = jnp.zeros((chunk, TB), jnp.float32)
        return carry

    lax.fori_loop(0, rows // chunk, start_rows, 0)
    gram_inv[...] = jnp.zeros_like(gram_inv)
    curv_old[...] = jnp.zeros_like(curv_old)

    def halo(it):
        to_right = pltpu.make_async_remote_copy(
            src_ref=vext.at[it, pl.ds(rows, HALO), :],
            dst_ref=vext.at[it, pl.ds(0, HALO), :],
            send_sem=halo_send.at[2 * it], recv_sem=halo_recv.at[2 * it],
            device_id=right, device_id_type=MESH,
        )
        to_left = pltpu.make_async_remote_copy(
            src_ref=vext.at[it, pl.ds(HALO, HALO), :],
            dst_ref=vext.at[it, pl.ds(HALO + rows, HALO), :],
            send_sem=halo_send.at[2 * it + 1], recv_sem=halo_recv.at[2 * it + 1],
            device_id=left, device_id_type=MESH,
        )
        return to_right, to_left

    pl.semaphore_wait(barrier, len(others))
    for copy in halo(0):
        copy.start()

    def iteration(it, carry):
        def apply_block(b, inner):
            at = pl.multiple_of(b * TB, TB)
            product = mm(band_ref[pl.ds(at, TB), :], vext[it, pl.ds(at, SPAN * TB), :])
            mine = pl.ds(at, TB)
            wbuf[mine, :] = r_ref[mine, :] - ALPHA * inv_ref[mine, :] * product
            return inner

        lax.fori_loop(BAND, blocks - BAND, apply_block, 0)

        @pl.when(it > 0)
        def _():
            gram_inv[...] = total[0:TB, :]
            invert_in_place(gram_inv)

        for copy in halo(it):
            copy.wait()
        lax.fori_loop(0, BAND, apply_block, 0)
        lax.fori_loop(blocks - BAND, blocks, apply_block, 0)

        acc[...] = jnp.zeros_like(acc)

        def add_gram(c, inner):
            at = pl.ds(pl.multiple_of(c * chunk, chunk), chunk)
            part = r_ref[at, :]
            both = mm_t(part, jnp.concatenate([part, wbuf[at, :]], axis=1))
            acc[0:TB, :] += both[:, 0:TB]
            acc[TB : 2 * TB, :] += both[:, TB : 2 * TB]
            return inner

        lax.fori_loop(0, rows // chunk, add_gram, 0)

        own = pl.ds(pl.multiple_of(node * share, share), share)
        copies = []
        for k in range(1, nodes):
            spot = it * nodes + k
            copy = pltpu.make_async_remote_copy(
                src_ref=acc.at[pl.ds(pl.multiple_of(node_at(k) * share, share), share), :],
                dst_ref=spread.at[spot],
                send_sem=spread_send.at[spot], recv_sem=spread_recv.at[spot],
                device_id=(node_at(k), col), device_id_type=MESH,
            )
            copy.start()
            copies.append(copy)
        for copy in copies:
            copy.wait()
        mine = acc[own, :]
        for k in range(1, nodes):
            mine = mine + spread[it * nodes + k]
        column_sums[it * cols + col] = mine
        copies = []
        for k in range(1, cols):
            spot = it * cols + k
            copy = pltpu.make_async_remote_copy(
                src_ref=column_sums.at[it * cols + col],
                dst_ref=column_sums.at[it * cols + col],
                send_sem=col_send.at[spot], recv_sem=col_recv.at[spot],
                device_id=(node, col_at(k)), device_id_type=MESH,
            )
            copy.start()
            copies.append(copy)
        for copy in copies:
            copy.wait()
        mine = column_sums[it * cols]
        for k in range(1, cols):
            mine = mine + column_sums[it * cols + k]
        total[own, :] = mine
        copies = []
        for k in range(1, nodes):
            spot = it * nodes + k
            copy = pltpu.make_async_remote_copy(
                src_ref=total.at[own, :],
                dst_ref=total.at[own, :],
                send_sem=back_send.at[spot], recv_sem=back_recv.at[spot],
                device_id=(node_at(k), col), device_id_type=MESH,
            )
            copy.start()
            copies.append(copy)
        for copy in copies:
            copy.wait()

        gram = total[0:TB, :]
        ratio = mm(gram_inv[...], gram)
        ratio_ref[...] = ratio
        curvature = total[TB : 2 * TB, :] - mm_t(ratio, mm(curv_old[...], ratio))
        curv_old[...] = curvature
        curv_inv[...] = curvature
        invert_in_place(curv_inv)
        step_ref[...] = mm(curv_inv[...], total[0:TB, :])

        def update_rows(c, inner):
            start = pl.multiple_of(c * chunk, chunk)
            at = pl.ds(start, chunk)
            fresh = r_ref[at, :] + mm(direc[at, :], ratio_ref[...])
            direc[at, :] = fresh
            x_ref[at, :] += mm(fresh, step_ref[...])
            turned = wbuf[at, :] + mm(image[at, :], ratio_ref[...])
            image[at, :] = turned
            left_over = r_ref[at, :] - mm(turned, step_ref[...])
            r_ref[at, :] = left_over
            vext[it + 1, pl.ds(HALO + start, chunk), :] = inv_ref[at, :] * left_over
            return inner

        edge = HALO // chunk
        lax.fori_loop(0, edge, update_rows, 0)
        lax.fori_loop(rows // chunk - edge, rows // chunk, update_rows, 0)

        @pl.when(it < ITERS - 1)
        def _():
            for copy in halo(it + 1):
                copy.start()

        lax.fori_loop(edge, rows // chunk - edge, update_rows, 0)
        return carry

    lax.fori_loop(0, ITERS, iteration, 0)


def run_cg(nodes, cols, prior, queries, band, inv):
    rows = prior.shape[0]
    share = 2 * TB // nodes
    full = pl.BlockSpec(memory_space=pltpu.VMEM)
    shape = jax.ShapeDtypeStruct((rows, TB), jnp.float32)
    big = pltpu.VMEM((rows, TB), jnp.float32)
    small = pltpu.VMEM((TB, TB), jnp.float32)
    tall = pltpu.VMEM((2 * TB, TB), jnp.float32)
    return pl.pallas_call(
        functools.partial(cg_kernel, nodes, cols),
        in_specs=[full] * 4,
        out_specs=[full] * 2,
        out_shape=[shape, shape],
        scratch_shapes=[
            pltpu.VMEM((ITERS + 1, rows + 2 * HALO, TB), jnp.float32),
            big, big, big, tall,
            pltpu.VMEM((ITERS * nodes, share, TB), jnp.float32),
            pltpu.VMEM((ITERS * cols, share, TB), jnp.float32),
            tall, small, small, small, small, small,
        ]
        + [pltpu.SemaphoreType.DMA((2 * ITERS,))] * 2
        + [pltpu.SemaphoreType.DMA((ITERS * nodes,))] * 2
        + [pltpu.SemaphoreType.DMA((ITERS * cols,))] * 2
        + [pltpu.SemaphoreType.DMA((ITERS * nodes,))] * 2,
        compiler_params=pltpu.CompilerParams(
            collective_id=0, has_side_effects=True, vmem_limit_bytes=56 * 1024 * 1024
        ),
    )(prior, queries, band, inv)


def body(prior, queries, tile_rows, tile_cols, tile_ids, tile_weights):
    rows_dev = prior.shape[0]
    nodes = lax.axis_size("nodes")
    cols = lax.axis_size("cols")
    node = lax.axis_index("nodes")
    member = lax.axis_index("cols")
    per_dev = tile_rows.shape[0]
    row_blocks = rows_dev // TB
    blocks = row_blocks * cols
    first = node * blocks

    keys = jnp.where(
        tile_rows >= 0, (tile_rows - first) * SPAN + (tile_cols - tile_rows + BAND), -1
    ).astype(jnp.float32)
    packed = jnp.concatenate([tile_ids.astype(jnp.float32), tile_weights], axis=1)
    meta_rows = 8 * (-(-per_dev // (8 * TB)))
    meta = jnp.full((meta_rows * TB,), -1.0, jnp.float32).at[:per_dev].set(keys)
    flat = jnp.concatenate([packed.reshape(per_dev * 2 * KT, TB), meta.reshape(meta_rows, TB)])
    gathered = lax.all_gather(flat, "cols", axis=0, tiled=False)
    stride = flat.shape[0]
    slot_keys = gathered[:, per_dev * 2 * KT :, :].reshape(cols, -1)[:, :per_dev].reshape(-1).astype(jnp.int32)
    slot = jnp.arange(cols * per_dev, dtype=jnp.int32)
    slot_at = (slot // per_dev) * stride + (slot % per_dev) * 2 * KT

    def find(wanted):
        return jnp.max(
            jnp.where(wanted[:, None] == slot_keys[None, :], slot_at[None, :], -1), axis=1
        )

    far = [a for a in range(BAND) for _ in range(a + 1)]
    near = [c for a in range(BAND) for c in range(a + 1)]
    far = jnp.array(far, jnp.int32)
    near = jnp.array(near, jnp.int32)
    up_keys = (blocks - BAND + far) * SPAN + (2 * BAND + near - far)
    down_keys = near * SPAN + (far - near)
    group_tiles = gathered.reshape(cols * stride, TB)

    def pick(wanted):
        at = find(wanted)
        found = jnp.maximum(at, 0)[:, None] + jnp.arange(2 * KT, dtype=jnp.int32)[None, :]
        chosen = group_tiles[found]
        return jnp.where((at >= 0)[:, None, None], chosen, 0.0).reshape(EDGE * 2 * KT, TB)

    from_prev = lax.ppermute(pick(up_keys), "nodes", [(i, i + 1) for i in range(nodes - 1)])
    from_next = lax.ppermute(pick(down_keys), "nodes", [(i + 1, i) for i in range(nodes - 1)])
    tiles = jnp.concatenate([group_tiles, from_prev, from_next])

    place = jnp.arange(row_blocks * SPAN, dtype=jnp.int32)
    i_at = member * row_blocks + place // SPAN
    o_at = place % SPAN
    forward = find(i_at * SPAN + o_at)
    back_row = i_at + o_at - BAND
    inside = find(back_row * SPAN + 2 * BAND - o_at)
    edge_at = cols * stride
    a_prev = back_row + BAND
    prev_at = edge_at + (a_prev * (a_prev + 1) // 2 + i_at) * 2 * KT
    c_next = i_at - (blocks - BAND)
    next_at = edge_at + (EDGE + c_next * (c_next + 1) // 2 + back_row - blocks) * 2 * KT
    backward = jnp.where(back_row < 0, prev_at, jnp.where(back_row >= blocks, next_at, inside))
    band, inv = build_band(jnp.stack([forward, backward]), tiles, row_blocks)
    return tuple(run_cg(nodes, cols, prior, queries[None, :], band, inv))


def solution(mesh):
    in_specs = (
        P(("nodes", "cols"), None),
        P(),
        P(("nodes", "cols")),
        P(("nodes", "cols")),
        P(("nodes", "cols"), None, None),
        P(("nodes", "cols"), None, None),
    )
    out_specs = (P(("nodes", "cols"), None), P(("nodes", "cols"), None))
    return jax.shard_map(body, mesh=mesh, in_specs=in_specs, out_specs=out_specs, check_vma=False)
```

```python
import functools

import jax
import jax.numpy as jnp
from jax import lax
from jax.experimental import pallas as pl
from jax.experimental.pallas import tpu as pltpu
from jax.sharding import PartitionSpec as P

TB = 128
KT = 8
BAND = 4
ITERS = 3
SPAN = 2 * BAND + 1
HALO = BAND * TB
EDGE = BAND * (BAND + 1) // 2

HIGH = lax.Precision.HIGHEST
ALPHA = 0.9
BOOST = 4.0
MESH = pl.DeviceIdType.MESH


def mm(left, right):
    return jnp.dot(left, right, precision=HIGH, preferred_element_type=jnp.float32)


def mm_t(left, right):
    return lax.dot_general(
        left, right, (((0,), (0,)), ((), ())), precision=HIGH, preferred_element_type=jnp.float32
    )


def split(value):
    high = value.astype(jnp.bfloat16)
    return high, (value - high.astype(jnp.float32)).astype(jnp.bfloat16)


def dot16(left, right, dim):
    return lax.dot_general(
        left, right, (((dim,), (0,)), ((), ())), preferred_element_type=jnp.float32
    )


def mm_pair(left_high, left_low, right):
    right_high, right_low = split(right)
    wide = dot16(left_high, jnp.concatenate([right_high, right_low], axis=1), 1)
    return wide[:, :TB] + (wide[:, TB:] + dot16(left_low, right_high, 1))


def mm_split(left, right):
    return mm_pair(*split(left), right)


def mm_t_split(left, right):
    left_high, left_low = split(left)
    right_high, right_low = split(right)
    return dot16(left_high, right_high, 0) + (
        dot16(left_high, right_low, 0) + dot16(left_low, right_high, 0)
    )


def band_kernel(offsets, tiles_ref, high_ref, low_ref, inv_ref, band_ref):
    row = pl.program_id(0)
    places = lax.broadcasted_iota(jnp.int32, (TB, TB), 0).astype(jnp.float32)

    def transposed_tile(offset):
        at = pl.multiple_of(offset, 8)
        ids = tiles_ref[pl.ds(at, KT), :]
        weights = tiles_ref[pl.ds(at + KT, KT), :]
        total = jnp.zeros((TB, TB), jnp.float32)
        for k in range(KT):
            total = total + jnp.where(ids[k : k + 1, :] == places, weights[k : k + 1, :], 0.0)
        return total

    for o in range(SPAN):
        forward = offsets[0, row * SPAN + o]
        backward = offsets[1, row * SPAN + o]
        lanes = slice(o * TB, (o + 1) * TB)

        @pl.when(forward >= 0)
        def _():
            band_ref[:, lanes] = transposed_tile(forward).T

        @pl.when(forward < 0)
        def _():
            band_ref[:, lanes] = jnp.zeros((TB, TB), jnp.float32)

        @pl.when(backward >= 0)
        def _():
            band_ref[:, lanes] += transposed_tile(backward)

    high_ref[...], low_ref[...] = split(band_ref[...])
    folded = band_ref[:, 0:TB]
    for o in range(1, SPAN):
        folded = folded + band_ref[:, o * TB : (o + 1) * TB]
    degree = jnp.broadcast_to(jnp.sum(folded, axis=1, keepdims=True), (TB, TB))
    root = lax.rsqrt(degree)
    inv_ref[...] = root * (1.5 - 0.5 * degree * root * root)


def build_band(offsets, tiles, row_blocks):
    return pl.pallas_call(
        band_kernel,
        grid_spec=pltpu.PrefetchScalarGridSpec(
            num_scalar_prefetch=1,
            grid=(row_blocks,),
            in_specs=[pl.BlockSpec(tiles.shape, lambda i, _: (0, 0))],
            out_specs=[
                pl.BlockSpec((TB, SPAN * TB), lambda i, _: (i, 0)),
                pl.BlockSpec((TB, SPAN * TB), lambda i, _: (i, 0)),
                pl.BlockSpec((TB, TB), lambda i, _: (i, 0)),
            ],
            scratch_shapes=[pltpu.VMEM((TB, SPAN * TB), jnp.float32)],
        ),
        out_shape=[
            jax.ShapeDtypeStruct((row_blocks * TB, SPAN * TB), jnp.bfloat16),
            jax.ShapeDtypeStruct((row_blocks * TB, SPAN * TB), jnp.bfloat16),
            jax.ShapeDtypeStruct((row_blocks * TB, TB), jnp.float32),
        ],
        compiler_params=pltpu.CompilerParams(vmem_limit_bytes=32 * 1024 * 1024),
    )(offsets, tiles)


def invert_in_place(matrix):
    lane = lax.broadcasted_iota(jnp.int32, (TB, TB), 1)
    lane_row = lax.broadcasted_iota(jnp.int32, (1, TB), 1)

    def entry(line, k):
        return jnp.sum(jnp.where(lane_row == k, line, 0.0), axis=1, keepdims=True)

    def pivot(m, carry):
        k = 2 * m
        whole = matrix[...]
        first = matrix[pl.ds(k, 1), :]
        second = matrix[pl.ds(k + 1, 1), :]
        hit0 = lane == k
        hit1 = lane == k + 1
        column0 = jnp.sum(jnp.where(hit0, whole, 0.0), axis=1, keepdims=True)
        column1 = jnp.sum(jnp.where(hit1, whole, 0.0), axis=1, keepdims=True)
        rest = jnp.where(hit0 | hit1, 0.0, whole)
        a = entry(first, k)
        b = entry(first, k + 1)
        c = entry(second, k)
        d = entry(second, k + 1)
        inv_a = 1.0 / a
        lower = c * inv_a
        upper = b * inv_a
        inv_s = 1.0 / (d - c * upper)
        row0 = jnp.where(lane_row == k, 1.0, jnp.where(lane_row == k + 1, 0.0, first))
        row1 = jnp.where(lane_row == k, 0.0, jnp.where(lane_row == k + 1, 1.0, second))
        new1 = (row1 - lower * row0) * inv_s
        new0 = row0 * inv_a - upper * new1
        matrix[...] = rest - column0 * new0 - column1 * new1
        matrix[pl.ds(k, 1), :] = new0
        matrix[pl.ds(k + 1, 1), :] = new1
        return carry

    lax.fori_loop(0, TB // 2, pivot, 0)


def cg_kernel(
    nodes, cols, prior_ref, queries_ref, high_ref, low_ref, inv_ref, x_ref, r_ref,
    vext, direc, image, wbuf, acc, spread, column_sums, total, gram_inv, curv_inv, curv_old,
    ratio_ref, step_ref, halo_send, halo_recv, spread_send, spread_recv, col_send, col_recv,
    back_send, back_recv,
):
    rows = prior_ref.shape[0]
    blocks = rows // TB
    node = lax.axis_index("nodes")
    col = lax.axis_index("cols")
    right = ((node + (col + 1) // cols) % nodes, (col + 1) % cols)
    left = ((node + nodes - 1 + (col + cols - 1) // cols) % nodes, (col + cols - 1) % cols)
    share = 2 * TB // nodes

    def node_at(k):
        return (node + k) % nodes

    def col_at(k):
        return (col + k) % cols

    barrier = pltpu.get_barrier_semaphore()
    others = [left, right]
    others += [(node_at(k), col) for k in range(1, nodes)]
    others += [(node, col_at(k)) for k in range(1, cols)]
    for other in others:
        pl.semaphore_signal(barrier, inc=1, device_id=other, device_id_type=MESH)

    base = (node * cols + col) * rows
    chunk = 2 * TB

    def start_rows(c, carry):
        start = pl.multiple_of(c * chunk, chunk)
        at = pl.ds(start, chunk)
        where_at = base + c * chunk + lax.broadcasted_iota(jnp.int32, (chunk, TB), 0)
        target = prior_ref[at, :] + jnp.where(where_at == queries_ref[...], BOOST, 0.0)
        r_ref[at, :] = target
        vext[0, pl.ds(HALO + start, chunk), :] = inv_ref[at, :] * target
        x_ref[at, :] = jnp.zeros((chunk, TB), jnp.float32)
        direc[at, :] = jnp.zeros((chunk, TB), jnp.float32)
        image[at, :] = jnp.zeros((chunk, TB), jnp.float32)
        return carry

    lax.fori_loop(0, rows // chunk, start_rows, 0)
    gram_inv[...] = jnp.zeros_like(gram_inv)
    curv_old[...] = jnp.zeros_like(curv_old)

    def halo(it):
        to_right = pltpu.make_async_remote_copy(
            src_ref=vext.at[it, pl.ds(rows, HALO), :],
            dst_ref=vext.at[it, pl.ds(0, HALO), :],
            send_sem=halo_send.at[2 * it], recv_sem=halo_recv.at[2 * it],
            device_id=right, device_id_type=MESH,
        )
        to_left = pltpu.make_async_remote_copy(
            src_ref=vext.at[it, pl.ds(HALO, HALO), :],
            dst_ref=vext.at[it, pl.ds(HALO + rows, HALO), :],
            send_sem=halo_send.at[2 * it + 1], recv_sem=halo_recv.at[2 * it + 1],
            device_id=left, device_id_type=MESH,
        )
        return to_right, to_left

    pl.semaphore_wait(barrier, len(others))
    for copy in halo(0):
        copy.start()

    def iteration(it, carry):
        def apply_block(b, inner):
            at = pl.multiple_of(b * TB, TB)
            product = mm_pair(
                high_ref[pl.ds(at, TB), :], low_ref[pl.ds(at, TB), :], vext[it, pl.ds(at, SPAN * TB), :]
            )
            mine = pl.ds(at, TB)
            wbuf[mine, :] = r_ref[mine, :] - ALPHA * inv_ref[mine, :] * product
            return inner

        lax.fori_loop(BAND, blocks - BAND, apply_block, 0)

        @pl.when(it > 0)
        def _():
            gram_inv[...] = total[0:TB, :]
            invert_in_place(gram_inv)

        for copy in halo(it):
            copy.wait()
        lax.fori_loop(0, BAND, apply_block, 0)
        lax.fori_loop(blocks - BAND, blocks, apply_block, 0)

        acc[...] = jnp.zeros_like(acc)

        def add_gram(c, inner):
            at = pl.ds(pl.multiple_of(c * chunk, chunk), chunk)
            part = r_ref[at, :]
            both = mm_t_split(part, jnp.concatenate([part, wbuf[at, :]], axis=1))
            acc[0:TB, :] += both[:, 0:TB]
            acc[TB : 2 * TB, :] += both[:, TB : 2 * TB]
            return inner

        lax.fori_loop(0, rows // chunk, add_gram, 0)

        own = pl.ds(pl.multiple_of(node * share, share), share)
        copies = []
        for k in range(1, nodes):
            spot = it * nodes + k
            copy = pltpu.make_async_remote_copy(
                src_ref=acc.at[pl.ds(pl.multiple_of(node_at(k) * share, share), share), :],
                dst_ref=spread.at[spot],
                send_sem=spread_send.at[spot], recv_sem=spread_recv.at[spot],
                device_id=(node_at(k), col), device_id_type=MESH,
            )
            copy.start()
            copies.append(copy)
        for copy in copies:
            copy.wait()
        mine = acc[own, :]
        for k in range(1, nodes):
            mine = mine + spread[it * nodes + k]
        column_sums[it * cols + col] = mine
        copies = []
        for k in range(1, cols):
            spot = it * cols + k
            copy = pltpu.make_async_remote_copy(
                src_ref=column_sums.at[it * cols + col],
                dst_ref=column_sums.at[it * cols + col],
                send_sem=col_send.at[spot], recv_sem=col_recv.at[spot],
                device_id=(node, col_at(k)), device_id_type=MESH,
            )
            copy.start()
            copies.append(copy)
        for copy in copies:
            copy.wait()
        mine = column_sums[it * cols]
        for k in range(1, cols):
            mine = mine + column_sums[it * cols + k]
        total[own, :] = mine
        copies = []
        for k in range(1, nodes):
            spot = it * nodes + k
            copy = pltpu.make_async_remote_copy(
                src_ref=total.at[own, :],
                dst_ref=total.at[own, :],
                send_sem=back_send.at[spot], recv_sem=back_recv.at[spot],
                device_id=(node_at(k), col), device_id_type=MESH,
            )
            copy.start()
            copies.append(copy)
        for copy in copies:
            copy.wait()

        gram = total[0:TB, :]
        ratio = mm(gram_inv[...], gram)
        ratio_ref[...] = ratio
        curvature = total[TB : 2 * TB, :] - mm_t(ratio, mm(curv_old[...], ratio))
        curv_old[...] = curvature
        curv_inv[...] = curvature
        invert_in_place(curv_inv)
        step_ref[...] = mm(curv_inv[...], total[0:TB, :])

        def update_rows(c, inner):
            start = pl.multiple_of(c * chunk, chunk)
            at = pl.ds(start, chunk)
            fresh = r_ref[at, :] + mm_split(direc[at, :], ratio_ref[...])
            direc[at, :] = fresh
            x_ref[at, :] += mm_split(fresh, step_ref[...])
            turned = wbuf[at, :] + mm_split(image[at, :], ratio_ref[...])
            image[at, :] = turned
            left_over = r_ref[at, :] - mm_split(turned, step_ref[...])
            r_ref[at, :] = left_over
            vext[it + 1, pl.ds(HALO + start, chunk), :] = inv_ref[at, :] * left_over
            return inner

        edge = HALO // chunk
        lax.fori_loop(0, edge, update_rows, 0)
        lax.fori_loop(rows // chunk - edge, rows // chunk, update_rows, 0)

        @pl.when(it < ITERS - 1)
        def _():
            for copy in halo(it + 1):
                copy.start()

        lax.fori_loop(edge, rows // chunk - edge, update_rows, 0)
        return carry

    lax.fori_loop(0, ITERS, iteration, 0)


def run_cg(nodes, cols, prior, queries, high, low, inv):
    rows = prior.shape[0]
    share = 2 * TB // nodes
    full = pl.BlockSpec(memory_space=pltpu.VMEM)
    shape = jax.ShapeDtypeStruct((rows, TB), jnp.float32)
    big = pltpu.VMEM((rows, TB), jnp.float32)
    small = pltpu.VMEM((TB, TB), jnp.float32)
    tall = pltpu.VMEM((2 * TB, TB), jnp.float32)
    return pl.pallas_call(
        functools.partial(cg_kernel, nodes, cols),
        in_specs=[full] * 5,
        out_specs=[full] * 2,
        out_shape=[shape, shape],
        scratch_shapes=[
            pltpu.VMEM((ITERS + 1, rows + 2 * HALO, TB), jnp.float32),
            big, big, big, tall,
            pltpu.VMEM((ITERS * nodes, share, TB), jnp.float32),
            pltpu.VMEM((ITERS * cols, share, TB), jnp.float32),
            tall, small, small, small, small, small,
        ]
        + [pltpu.SemaphoreType.DMA((2 * ITERS,))] * 2
        + [pltpu.SemaphoreType.DMA((ITERS * nodes,))] * 2
        + [pltpu.SemaphoreType.DMA((ITERS * cols,))] * 2
        + [pltpu.SemaphoreType.DMA((ITERS * nodes,))] * 2,
        compiler_params=pltpu.CompilerParams(
            collective_id=0, has_side_effects=True, vmem_limit_bytes=56 * 1024 * 1024
        ),
    )(prior, queries, high, low, inv)


def body(prior, queries, tile_rows, tile_cols, tile_ids, tile_weights):
    rows_dev = prior.shape[0]
    nodes = lax.axis_size("nodes")
    cols = lax.axis_size("cols")
    node = lax.axis_index("nodes")
    member = lax.axis_index("cols")
    per_dev = tile_rows.shape[0]
    row_blocks = rows_dev // TB
    blocks = row_blocks * cols
    first = node * blocks

    keys = jnp.where(
        tile_rows >= 0, (tile_rows - first) * SPAN + (tile_cols - tile_rows + BAND), -1
    ).astype(jnp.float32)
    packed = jnp.concatenate([tile_ids.astype(jnp.float32), tile_weights], axis=1)
    meta_rows = 8 * (-(-per_dev // (8 * TB)))
    meta = jnp.full((meta_rows * TB,), -1.0, jnp.float32).at[:per_dev].set(keys)
    flat = jnp.concatenate([packed.reshape(per_dev * 2 * KT, TB), meta.reshape(meta_rows, TB)])
    gathered = lax.all_gather(flat, "cols", axis=0, tiled=False)
    stride = flat.shape[0]
    slot_keys = gathered[:, per_dev * 2 * KT :, :].reshape(cols, -1)[:, :per_dev].reshape(-1).astype(jnp.int32)
    slot = jnp.arange(cols * per_dev, dtype=jnp.int32)
    slot_at = (slot // per_dev) * stride + (slot % per_dev) * 2 * KT

    def find(wanted):
        return jnp.max(
            jnp.where(wanted[:, None] == slot_keys[None, :], slot_at[None, :], -1), axis=1
        )

    far = [a for a in range(BAND) for _ in range(a + 1)]
    near = [c for a in range(BAND) for c in range(a + 1)]
    far = jnp.array(far, jnp.int32)
    near = jnp.array(near, jnp.int32)
    up_keys = (blocks - BAND + far) * SPAN + (2 * BAND + near - far)
    down_keys = near * SPAN + (far - near)
    group_tiles = gathered.reshape(cols * stride, TB)

    def pick(wanted):
        at = find(wanted)
        found = jnp.maximum(at, 0)[:, None] + jnp.arange(2 * KT, dtype=jnp.int32)[None, :]
        chosen = group_tiles[found]
        return jnp.where((at >= 0)[:, None, None], chosen, 0.0).reshape(EDGE * 2 * KT, TB)

    from_prev = lax.ppermute(pick(up_keys), "nodes", [(i, i + 1) for i in range(nodes - 1)])
    from_next = lax.ppermute(pick(down_keys), "nodes", [(i + 1, i) for i in range(nodes - 1)])
    tiles = jnp.concatenate([group_tiles, from_prev, from_next])

    place = jnp.arange(row_blocks * SPAN, dtype=jnp.int32)
    i_at = member * row_blocks + place // SPAN
    o_at = place % SPAN
    forward = find(i_at * SPAN + o_at)
    back_row = i_at + o_at - BAND
    inside = find(back_row * SPAN + 2 * BAND - o_at)
    edge_at = cols * stride
    a_prev = back_row + BAND
    prev_at = edge_at + (a_prev * (a_prev + 1) // 2 + i_at) * 2 * KT
    c_next = i_at - (blocks - BAND)
    next_at = edge_at + (EDGE + c_next * (c_next + 1) // 2 + back_row - blocks) * 2 * KT
    backward = jnp.where(back_row < 0, prev_at, jnp.where(back_row >= blocks, next_at, inside))
    high, low, inv = build_band(jnp.stack([forward, backward]), tiles, row_blocks)
    return tuple(run_cg(nodes, cols, prior, queries[None, :], high, low, inv))


def solution(mesh):
    in_specs = (
        P(("nodes", "cols"), None),
        P(),
        P(("nodes", "cols")),
        P(("nodes", "cols")),
        P(("nodes", "cols"), None, None),
        P(("nodes", "cols"), None, None),
    )
    out_specs = (P(("nodes", "cols"), None), P(("nodes", "cols"), None))
    return jax.shard_map(body, mesh=mesh, in_specs=in_specs, out_specs=out_specs, check_vma=False)
```

```python
import functools

import jax
import jax.numpy as jnp
from jax import lax
from jax.experimental import pallas as pl
from jax.experimental.pallas import tpu as pltpu
from jax.sharding import PartitionSpec as P

TB = 128
KT = 8
BAND = 4
ITERS = 3
SPAN = 2 * BAND + 1
HALO = BAND * TB
EDGE = BAND * (BAND + 1) // 2

HIGH = lax.Precision.HIGHEST
ALPHA = 0.9
BOOST = 4.0
MESH = pl.DeviceIdType.MESH


def mm(left, right):
    return jnp.dot(left, right, precision=HIGH, preferred_element_type=jnp.float32)


def mm_t(left, right):
    return lax.dot_general(
        left, right, (((0,), (0,)), ((), ())), precision=HIGH, preferred_element_type=jnp.float32
    )


def split(value):
    high = value.astype(jnp.bfloat16)
    return high, (value - high.astype(jnp.float32)).astype(jnp.bfloat16)


def dot16(left, right, dim):
    return lax.dot_general(
        left, right, (((dim,), (0,)), ((), ())), preferred_element_type=jnp.float32
    )


def mm_pair(left_high, left_low, right):
    right_high, right_low = split(right)
    wide = dot16(left_high, jnp.concatenate([right_high, right_low], axis=1), 1)
    return wide[:, :TB] + (wide[:, TB:] + dot16(left_low, right_high, 1))


def mm_split(left, right):
    return mm_pair(*split(left), right)


def mm_t_split(left, right):
    left_high, left_low = split(left)
    right_high, right_low = split(right)
    return dot16(left_high, right_high, 0) + (
        dot16(left_high, right_low, 0) + dot16(left_low, right_high, 0)
    )


def band_kernel(offsets, tiles_ref, high_ref, low_ref, inv_ref, band_ref):
    row = pl.program_id(0)
    places = lax.broadcasted_iota(jnp.int32, (TB, TB), 0).astype(jnp.float32)

    def transposed_tile(offset):
        at = pl.multiple_of(offset, 8)
        ids = tiles_ref[pl.ds(at, KT), :]
        weights = tiles_ref[pl.ds(at + KT, KT), :]
        total = jnp.zeros((TB, TB), jnp.float32)
        for k in range(KT):
            total = total + jnp.where(ids[k : k + 1, :] == places, weights[k : k + 1, :], 0.0)
        return total

    for o in range(SPAN):
        forward = offsets[0, row * SPAN + o]
        backward = offsets[1, row * SPAN + o]
        lanes = slice(o * TB, (o + 1) * TB)

        @pl.when(forward >= 0)
        def _():
            band_ref[:, lanes] = transposed_tile(forward).T

        @pl.when(forward < 0)
        def _():
            band_ref[:, lanes] = jnp.zeros((TB, TB), jnp.float32)

        @pl.when(backward >= 0)
        def _():
            band_ref[:, lanes] += transposed_tile(backward)

    high_ref[...], low_ref[...] = split(band_ref[...])
    folded = band_ref[:, 0:TB]
    for o in range(1, SPAN):
        folded = folded + band_ref[:, o * TB : (o + 1) * TB]
    degree = jnp.broadcast_to(jnp.sum(folded, axis=1, keepdims=True), (TB, TB))
    root = lax.rsqrt(degree)
    inv_ref[...] = root * (1.5 - 0.5 * degree * root * root)


def build_band(offsets, tiles, row_blocks):
    return pl.pallas_call(
        band_kernel,
        grid_spec=pltpu.PrefetchScalarGridSpec(
            num_scalar_prefetch=1,
            grid=(row_blocks,),
            in_specs=[pl.BlockSpec(tiles.shape, lambda i, _: (0, 0))],
            out_specs=[
                pl.BlockSpec((TB, SPAN * TB), lambda i, _: (i, 0)),
                pl.BlockSpec((TB, SPAN * TB), lambda i, _: (i, 0)),
                pl.BlockSpec((TB, TB), lambda i, _: (i, 0)),
            ],
            scratch_shapes=[pltpu.VMEM((TB, SPAN * TB), jnp.float32)],
        ),
        out_shape=[
            jax.ShapeDtypeStruct((row_blocks * TB, SPAN * TB), jnp.bfloat16),
            jax.ShapeDtypeStruct((row_blocks * TB, SPAN * TB), jnp.bfloat16),
            jax.ShapeDtypeStruct((row_blocks * TB, TB), jnp.float32),
        ],
        compiler_params=pltpu.CompilerParams(vmem_limit_bytes=32 * 1024 * 1024),
    )(offsets, tiles)


def invert_in_place(matrix):
    lane = lax.broadcasted_iota(jnp.int32, (TB, TB), 1)
    lane_row = lax.broadcasted_iota(jnp.int32, (1, TB), 1)

    def entry(line, k):
        return jnp.sum(jnp.where(lane_row == k, line, 0.0), axis=1, keepdims=True)

    def pivot(m, carry):
        k = 2 * m
        whole = matrix[...]
        first = matrix[pl.ds(k, 1), :]
        second = matrix[pl.ds(k + 1, 1), :]
        hit0 = lane == k
        hit1 = lane == k + 1
        column0 = jnp.sum(jnp.where(hit0, whole, 0.0), axis=1, keepdims=True)
        column1 = jnp.sum(jnp.where(hit1, whole, 0.0), axis=1, keepdims=True)
        rest = jnp.where(hit0 | hit1, 0.0, whole)
        a = entry(first, k)
        b = entry(first, k + 1)
        c = entry(second, k)
        d = entry(second, k + 1)
        inv_a = 1.0 / a
        lower = c * inv_a
        upper = b * inv_a
        inv_s = 1.0 / (d - c * upper)
        row0 = jnp.where(lane_row == k, 1.0, jnp.where(lane_row == k + 1, 0.0, first))
        row1 = jnp.where(lane_row == k, 0.0, jnp.where(lane_row == k + 1, 1.0, second))
        new1 = (row1 - lower * row0) * inv_s
        new0 = row0 * inv_a - upper * new1
        matrix[...] = rest - column0 * new0 - column1 * new1
        matrix[pl.ds(k, 1), :] = new0
        matrix[pl.ds(k + 1, 1), :] = new1
        return carry

    lax.fori_loop(0, TB // 2, pivot, 0)


def cg_kernel(
    nodes, cols, prior_ref, queries_ref, high_ref, low_ref, inv_ref, x_ref, r_ref,
    vext, direc, image, wbuf, acc, spread, column_sums, total, gram_inv, curv_inv, curv_old,
    ratio_ref, step_ref, halo_send, halo_recv, spread_send, spread_recv, col_send, col_recv,
    back_send, back_recv,
):
    rows = prior_ref.shape[0]
    blocks = rows // TB
    node = lax.axis_index("nodes")
    col = lax.axis_index("cols")
    right = ((node + (col + 1) // cols) % nodes, (col + 1) % cols)
    left = ((node + nodes - 1 + (col + cols - 1) // cols) % nodes, (col + cols - 1) % cols)
    share = 2 * TB // nodes

    def node_at(k):
        return (node + k) % nodes

    def col_at(k):
        return (col + k) % cols

    barrier = pltpu.get_barrier_semaphore()
    others = [left, right]
    others += [(node_at(k), col) for k in range(1, nodes)]
    others += [(node, col_at(k)) for k in range(1, cols)]
    for other in others:
        pl.semaphore_signal(barrier, inc=1, device_id=other, device_id_type=MESH)

    base = (node * cols + col) * rows
    chunk = 2 * TB

    def start_rows(c, carry):
        start = pl.multiple_of(c * chunk, chunk)
        at = pl.ds(start, chunk)
        where_at = base + c * chunk + lax.broadcasted_iota(jnp.int32, (chunk, TB), 0)
        target = prior_ref[at, :] + jnp.where(where_at == queries_ref[...], BOOST, 0.0)
        r_ref[at, :] = target
        vext[0, pl.ds(HALO + start, chunk), :] = inv_ref[at, :] * target
        x_ref[at, :] = jnp.zeros((chunk, TB), jnp.float32)
        direc[at, :] = jnp.zeros((chunk, TB), jnp.float32)
        image[at, :] = jnp.zeros((chunk, TB), jnp.float32)
        return carry

    lax.fori_loop(0, rows // chunk, start_rows, 0)
    gram_inv[...] = jnp.zeros_like(gram_inv)
    curv_old[...] = jnp.zeros_like(curv_old)

    def halo(it):
        to_right = pltpu.make_async_remote_copy(
            src_ref=vext.at[it, pl.ds(rows, HALO), :],
            dst_ref=vext.at[it, pl.ds(0, HALO), :],
            send_sem=halo_send.at[2 * it], recv_sem=halo_recv.at[2 * it],
            device_id=right, device_id_type=MESH,
        )
        to_left = pltpu.make_async_remote_copy(
            src_ref=vext.at[it, pl.ds(HALO, HALO), :],
            dst_ref=vext.at[it, pl.ds(HALO + rows, HALO), :],
            send_sem=halo_send.at[2 * it + 1], recv_sem=halo_recv.at[2 * it + 1],
            device_id=left, device_id_type=MESH,
        )
        return to_right, to_left

    pl.semaphore_wait(barrier, len(others))
    for copy in halo(0):
        copy.start()

    def iteration(it, carry):
        def apply_block(b, inner):
            at = pl.multiple_of(b * TB, TB)
            product = mm_pair(
                high_ref[pl.ds(at, TB), :], low_ref[pl.ds(at, TB), :], vext[it, pl.ds(at, SPAN * TB), :]
            )
            mine = pl.ds(at, TB)
            wbuf[mine, :] = r_ref[mine, :] - ALPHA * inv_ref[mine, :] * product
            return inner

        lax.fori_loop(BAND, blocks - BAND, apply_block, 0)

        @pl.when(it > 0)
        def _():
            gram_inv[...] = total[0:TB, :]
            invert_in_place(gram_inv)

        for copy in halo(it):
            copy.wait()
        lax.fori_loop(0, BAND, apply_block, 0)
        lax.fori_loop(blocks - BAND, blocks, apply_block, 0)

        acc[...] = jnp.zeros_like(acc)

        def add_gram(c, inner):
            at = pl.ds(pl.multiple_of(c * chunk, chunk), chunk)
            part = r_ref[at, :]
            both = mm_t_split(part, jnp.concatenate([part, wbuf[at, :]], axis=1))
            acc[0:TB, :] += both[:, 0:TB]
            acc[TB : 2 * TB, :] += both[:, TB : 2 * TB]
            return inner

        lax.fori_loop(0, rows // chunk, add_gram, 0)

        own = pl.ds(pl.multiple_of(node * share, share), share)
        copies = []
        for k in range(1, nodes):
            spot = it * nodes + k
            copy = pltpu.make_async_remote_copy(
                src_ref=acc.at[pl.ds(pl.multiple_of(node_at(k) * share, share), share), :],
                dst_ref=spread.at[spot],
                send_sem=spread_send.at[spot], recv_sem=spread_recv.at[spot],
                device_id=(node_at(k), col), device_id_type=MESH,
            )
            copy.start()
            copies.append(copy)
        for copy in copies:
            copy.wait()
        mine = acc[own, :]
        for k in range(1, nodes):
            mine = mine + spread[it * nodes + k]
        column_sums[it * cols + col] = mine
        copies = []
        for k in range(1, cols):
            spot = it * cols + k
            copy = pltpu.make_async_remote_copy(
                src_ref=column_sums.at[it * cols + col],
                dst_ref=column_sums.at[it * cols + col],
                send_sem=col_send.at[spot], recv_sem=col_recv.at[spot],
                device_id=(node, col_at(k)), device_id_type=MESH,
            )
            copy.start()
            copies.append(copy)
        for copy in copies:
            copy.wait()
        mine = column_sums[it * cols]
        for k in range(1, cols):
            mine = mine + column_sums[it * cols + k]
        total[own, :] = mine
        copies = []
        for k in range(1, nodes):
            spot = it * nodes + k
            copy = pltpu.make_async_remote_copy(
                src_ref=total.at[own, :],
                dst_ref=total.at[own, :],
                send_sem=back_send.at[spot], recv_sem=back_recv.at[spot],
                device_id=(node_at(k), col), device_id_type=MESH,
            )
            copy.start()
            copies.append(copy)
        for copy in copies:
            copy.wait()

        gram = total[0:TB, :]
        ratio = mm(gram_inv[...], gram)
        ratio_ref[...] = ratio
        curvature = total[TB : 2 * TB, :] - mm_t(ratio, mm(curv_old[...], ratio))
        curv_old[...] = curvature
        curv_inv[...] = curvature
        invert_in_place(curv_inv)
        step_ref[...] = mm(curv_inv[...], total[0:TB, :])

        def update_rows(c, inner):
            start = pl.multiple_of(c * chunk, chunk)
            at = pl.ds(start, chunk)
            fresh = r_ref[at, :] + mm_split(direc[at, :], ratio_ref[...])
            direc[at, :] = fresh
            x_ref[at, :] += mm_split(fresh, step_ref[...])
            turned = wbuf[at, :] + mm_split(image[at, :], ratio_ref[...])
            image[at, :] = turned
            left_over = r_ref[at, :] - mm_split(turned, step_ref[...])
            r_ref[at, :] = left_over
            vext[it + 1, pl.ds(HALO + start, chunk), :] = inv_ref[at, :] * left_over
            return inner

        edge = HALO // chunk
        lax.fori_loop(0, edge, update_rows, 0)
        lax.fori_loop(rows // chunk - edge, rows // chunk, update_rows, 0)

        @pl.when(it < ITERS - 1)
        def _():
            for copy in halo(it + 1):
                copy.start()

        lax.fori_loop(edge, rows // chunk - edge, update_rows, 0)
        return carry

    lax.fori_loop(0, ITERS, iteration, 0)


def run_cg(nodes, cols, prior, queries, high, low, inv):
    rows = prior.shape[0]
    share = 2 * TB // nodes
    full = pl.BlockSpec(memory_space=pltpu.VMEM)
    shape = jax.ShapeDtypeStruct((rows, TB), jnp.float32)
    big = pltpu.VMEM((rows, TB), jnp.float32)
    small = pltpu.VMEM((TB, TB), jnp.float32)
    tall = pltpu.VMEM((2 * TB, TB), jnp.float32)
    return pl.pallas_call(
        functools.partial(cg_kernel, nodes, cols),
        in_specs=[full] * 5,
        out_specs=[full] * 2,
        out_shape=[shape, shape],
        scratch_shapes=[
            pltpu.VMEM((ITERS + 1, rows + 2 * HALO, TB), jnp.float32),
            big, big, big, tall,
            pltpu.VMEM((ITERS * nodes, share, TB), jnp.float32),
            pltpu.VMEM((ITERS * cols, share, TB), jnp.float32),
            tall, small, small, small, small, small,
        ]
        + [pltpu.SemaphoreType.DMA((2 * ITERS,))] * 2
        + [pltpu.SemaphoreType.DMA((ITERS * nodes,))] * 2
        + [pltpu.SemaphoreType.DMA((ITERS * cols,))] * 2
        + [pltpu.SemaphoreType.DMA((ITERS * nodes,))] * 2,
        compiler_params=pltpu.CompilerParams(
            collective_id=0, has_side_effects=True, vmem_limit_bytes=56 * 1024 * 1024
        ),
    )(prior, queries, high, low, inv)


def gather_kernel(cols, parts, shard_ref, out_ref, send_sem, recv_sem):
    node = lax.axis_index("nodes")
    col = lax.axis_index("cols")
    piece = shard_ref.shape[0] // parts
    barrier = pltpu.get_barrier_semaphore()
    for step in (1, cols - 1):
        pl.semaphore_signal(
            barrier, inc=1, device_id=(node, (col + step) % cols), device_id_type=MESH
        )
    out_ref[col] = shard_ref[...]
    pl.semaphore_wait(barrier, 2)

    def hop(way, h, p, source):
        at = pl.ds(p * piece, piece)
        target = (col + 1) % cols if way == 0 else (col + cols - 1) % cols
        return pltpu.make_async_remote_copy(
            src_ref=out_ref.at[source, at, :], dst_ref=out_ref.at[source, at, :],
            send_sem=send_sem.at[way, h, p], recv_sem=recv_sem.at[way, h, p],
            device_id=(node, target), device_id_type=MESH,
        )

    for h in range(cols):
        for p in range(parts):
            for way in range(2):
                source = col - h if way == 0 else col + h
                held = source >= 0 if way == 0 else source < cols
                onward = col < cols - 1 if way == 0 else col > 0
                if h > 0:

                    @pl.when(held)
                    def _():
                        hop(way, h - 1, p, source).wait_recv()

                if h < cols - 1:

                    @pl.when(held & onward)
                    def _():
                        hop(way, h, p, source).start()

    for h in range(cols - 1):
        for p in range(parts):
            for way in range(2):
                source = col - h if way == 0 else col + h
                held = source >= 0 if way == 0 else source < cols
                onward = col < cols - 1 if way == 0 else col > 0

                @pl.when(held & onward)
                def _():
                    hop(way, h, p, source).wait_send()


def gather_cols(cols, flat):
    parts = 3 if flat.shape[0] % 24 == 0 else 1
    full = pl.BlockSpec(memory_space=pltpu.VMEM)
    return pl.pallas_call(
        functools.partial(gather_kernel, cols, parts),
        in_specs=[full],
        out_specs=full,
        out_shape=jax.ShapeDtypeStruct((cols,) + flat.shape, flat.dtype),
        scratch_shapes=[pltpu.SemaphoreType.DMA((2, cols, parts))] * 2,
        compiler_params=pltpu.CompilerParams(
            collective_id=1, has_side_effects=True, vmem_limit_bytes=32 * 1024 * 1024
        ),
    )(flat)


def body(prior, queries, tile_rows, tile_cols, tile_ids, tile_weights):
    rows_dev = prior.shape[0]
    nodes = lax.axis_size("nodes")
    cols = lax.axis_size("cols")
    node = lax.axis_index("nodes")
    member = lax.axis_index("cols")
    per_dev = tile_rows.shape[0]
    row_blocks = rows_dev // TB
    blocks = row_blocks * cols
    first = node * blocks

    keys = jnp.where(
        tile_rows >= 0, (tile_rows - first) * SPAN + (tile_cols - tile_rows + BAND), -1
    ).astype(jnp.float32)
    packed = jnp.concatenate([tile_ids.astype(jnp.float32), tile_weights], axis=1)
    meta_rows = 8 * (-(-per_dev // (8 * TB)))
    meta = jnp.full((meta_rows * TB,), -1.0, jnp.float32).at[:per_dev].set(keys)
    flat = jnp.concatenate([packed.reshape(per_dev * 2 * KT, TB), meta.reshape(meta_rows, TB)])
    gathered = gather_cols(cols, flat)
    stride = flat.shape[0]
    slot_keys = gathered[:, per_dev * 2 * KT :, :].reshape(cols, -1)[:, :per_dev].reshape(-1).astype(jnp.int32)
    slot = jnp.arange(cols * per_dev, dtype=jnp.int32)
    slot_at = (slot // per_dev) * stride + (slot % per_dev) * 2 * KT

    def find(wanted):
        return jnp.max(
            jnp.where(wanted[:, None] == slot_keys[None, :], slot_at[None, :], -1), axis=1
        )

    far = [a for a in range(BAND) for _ in range(a + 1)]
    near = [c for a in range(BAND) for c in range(a + 1)]
    far = jnp.array(far, jnp.int32)
    near = jnp.array(near, jnp.int32)
    up_keys = (blocks - BAND + far) * SPAN + (2 * BAND + near - far)
    down_keys = near * SPAN + (far - near)
    group_tiles = gathered.reshape(cols * stride, TB)

    def pick(wanted):
        at = find(wanted)
        found = jnp.maximum(at, 0)[:, None] + jnp.arange(2 * KT, dtype=jnp.int32)[None, :]
        chosen = group_tiles[found]
        return jnp.where((at >= 0)[:, None, None], chosen, 0.0).reshape(EDGE * 2 * KT, TB)

    from_prev = lax.ppermute(pick(up_keys), "nodes", [(i, i + 1) for i in range(nodes - 1)])
    from_next = lax.ppermute(pick(down_keys), "nodes", [(i + 1, i) for i in range(nodes - 1)])
    tiles = jnp.concatenate([group_tiles, from_prev, from_next])

    place = jnp.arange(row_blocks * SPAN, dtype=jnp.int32)
    i_at = member * row_blocks + place // SPAN
    o_at = place % SPAN
    forward = find(i_at * SPAN + o_at)
    back_row = i_at + o_at - BAND
    inside = find(back_row * SPAN + 2 * BAND - o_at)
    edge_at = cols * stride
    a_prev = back_row + BAND
    prev_at = edge_at + (a_prev * (a_prev + 1) // 2 + i_at) * 2 * KT
    c_next = i_at - (blocks - BAND)
    next_at = edge_at + (EDGE + c_next * (c_next + 1) // 2 + back_row - blocks) * 2 * KT
    backward = jnp.where(back_row < 0, prev_at, jnp.where(back_row >= blocks, next_at, inside))
    high, low, inv = build_band(jnp.stack([forward, backward]), tiles, row_blocks)
    return tuple(run_cg(nodes, cols, prior, queries[None, :], high, low, inv))


def solution(mesh):
    in_specs = (
        P(("nodes", "cols"), None),
        P(),
        P(("nodes", "cols")),
        P(("nodes", "cols")),
        P(("nodes", "cols"), None, None),
        P(("nodes", "cols"), None, None),
    )
    out_specs = (P(("nodes", "cols"), None), P(("nodes", "cols"), None))
    return jax.shard_map(body, mesh=mesh, in_specs=in_specs, out_specs=out_specs, check_vma=False)
```
